32 devices in a mesh: grp: 2 (over y), seq: 4 (over z), smp: 2 (over x), rep: 2 (over core).
Axes of the slice: x: 2, y: 2, z: 4, core: 2. Of those that a mesh axis runs over, the one named last changes fastest.
Arguments:
- atom_single: bfloat16 [32, 512, 128], P(('grp', 'smp', 'rep'), 'seq'), parts along dimension 0, may hold values from -6 to 6
- token_counts: int32 [8, 16], P(('grp', 'seq')), parts along dimension 0, may hold values from 1 to 24, 128 in all within a row
- key_shift: int32 [32], P(('grp', 'seq')), parts along dimension 0, may hold values from -16 to 16, as said below
- atom_pair: bfloat16 [32, 16, 4096], P(('grp', 'seq')), parts along dimension 0, may hold values from -500 to 500
- project_weight: bfloat16 [4, 128, 128], replicated, may hold values from -0.5 to 0.5
- bias_weight: float32 [16, 4], replicated, may hold values from -1.5 to 1.5
- output_weight: bfloat16 [128, 128], replicated, may hold values from -0.5 to 0.5
- token_weight: bfloat16 [128, 768], replicated, may hold values from -0.5 to 0.5
- token_grad: bfloat16 [32, 64, 768], P(('grp', 'smp', 'rep'), 'seq'), parts along dimension 0, may hold values from -24 to 24
Outputs:
- single_grad: bfloat16 [32, 512, 128], P(('grp', 'smp', 'rep'), 'seq'), parts along dimension 0
- pair_grad: bfloat16 [32, 16, 4096], P(('grp', 'seq'), None, ('smp', 'rep')), parts along dimension 0
- token_weight_grad: float32 [256, 768], P('grp'), parts along dimension 0
- project_weight_grad: float32 [8, 128, 128], P('grp'), parts along dimension 0
The draws below stay inside these ranges and needn't reach their ends.
There are 2 independent parts, one for each index of `grp`. The reference program is written for one: setup_inputs(seed, part) draws one part's arguments, and reference() takes and returns one part's arrays. A program takes and returns all parts, laid end to end along the dimension named above; an argument that names none is the same for every part. Nothing has to cross between parts.
Inputs may be any that keep to these rules, and one draw needn't show every extreme that they name: `token_counts`: each row of 16 counts sums to 128: the atoms of a block of 128 atoms belong to the tokens of the same block, in token order. `key_shift`: each value is -16, 0 or 16; the first window's is -16 and the last window's is 16.
All inputs are finite; a program needn't handle non-finite values.
Results may differ from the reference program's by a relative error of at most 0.02.
Values may be sent and summed in bfloat16 or wider, within the bound.
A program may use at most 64 MiB of HBM per device.

```python
import math
import jax
import jax.numpy as jnp
import numpy as np
from jax import lax

C = 128
CP = 16
H = 4
HD = 32
CT = 768
QW = 32
KW = 128
JIT = 16
MOST = 24
ATOM_DEV = 128
HALO = 64
TOK_DEV = 16
SAMPLES = 16
NATOM = 512
NTOK = 64
NWIN = 16
N_SEQ = 4


def draw_key_shift(key, part):
    drawn = jax.random.randint(key, (NWIN,), 0, 3).astype(jnp.int32)
    shift_values = (drawn - 1) * JIT
    place = jnp.arange(NWIN, dtype=jnp.int32)
    shift_values = jnp.where(place == 0, -JIT, shift_values)
    shift_values = jnp.where(place == NWIN - 1, JIT, shift_values)
    return shift_values.astype(jnp.int32)


def draw_atom_pair(key, part):
    keys = jax.random.split(key, 7)
    shape = (NWIN, CP, QW * KW)
    values = jax.random.normal(keys[6], shape, jnp.float32)
    return jnp.clip(values, -4.0, 4.0).astype(jnp.bfloat16)


def shard_levels(rng, shape, shards, low, high):
    def one(axis_at, blocks):
        steps = jax.random.uniform(jax.random.fold_in(jax.random.fold_in(rng, 6), axis_at), (blocks,), jnp.float32, low / len(shards), high / len(shards))
        return jnp.repeat(jnp.exp(steps), shape[axis_at] // blocks).reshape((-1,) + (1,) * (len(shape) - axis_at - 1))

    loudness = one(*shards[0])
    for cut in shards[1:]:
        loudness = loudness * one(*cut)
    return loudness


def profile(amount, total, most, slope):
    portions = [(1 << 20) // math.isqrt(standing ** slope) + 1 for standing in range(2, amount + 1)]
    spare, counts = total - most - (amount - 1), [1] * (amount - 1)
    while spare > 0:
        candidates = [i for i in range(amount - 1) if counts[i] < most]
        mass, remaining = sum([portions[i] for i in candidates]), spare
        for i in candidates:
            extra = min(most - counts[i], max(1, remaining * portions[i] // mass), spare)
            counts[i] = counts[i] + extra
            spare = spare - extra
    return np.array([most] + counts)


def ragged_sizes(key, number_of, total, reach, slope):
    if number_of == 2:
        one = jax.random.randint(key, (), max(1, total - reach), min(reach, total - 1) + 1)
        return jnp.stack([one, total - one])
    lengths = jnp.asarray(profile(number_of, total, reach, slope), jnp.int32)
    couples = (number_of - 1) // 2
    giver, sink = lengths[1:1 + 2 * couples:2], lengths[2:2 + 2 * couples:2]
    room = jnp.minimum(giver - 1, reach - sink)
    moved = jax.random.randint(jax.random.fold_in(key, 1), (couples,), 0, 1 << 20) % (room + 1)
    lengths = lengths.at[1:1 + 2 * couples:2].set(giver - moved).at[2:2 + 2 * couples:2].set(sink + moved)
    return lengths[jax.random.permutation(jax.random.fold_in(key, 2), number_of)]


def scatter_about(key, extent, deviation, limit, shards=(), kind=jnp.bfloat16):
    array = deviation * jax.random.normal(key, extent, jnp.float32)
    if shards:
        array = array * shard_levels(key, extent, shards, -0.22, 0.18)
    return jnp.clip(array, -limit, limit).astype(kind)


def setup_inputs(seed: int = 0, part: int = 0) -> dict:
    seeds = jax.random.split(jax.random.key(seed), 10)
    own_keys = jax.random.split(jax.random.fold_in(seeds[9], part), 10)
    return {
        "atom_single": scatter_about(own_keys[0], (SAMPLES, NATOM, C), 1.0, 6.0, ((0, 4), (1, 4))),
        "token_counts": jax.vmap(lambda own: ragged_sizes(own, TOK_DEV, ATOM_DEV, MOST, 2))(jax.random.split(own_keys[1], N_SEQ)).reshape((N_SEQ, TOK_DEV)).astype(jnp.int32),
        "key_shift": draw_key_shift(jax.random.fold_in(jax.random.fold_in(seeds[9], part), 71), part),
        "atom_pair": draw_atom_pair(jax.random.fold_in(jax.random.fold_in(seeds[9], part), 71), part),
        "project_weight": scatter_about(seeds[4], (4, C, H * HD), C ** -0.5, 0.5),
        "bias_weight": scatter_about(seeds[5], (CP, H), CP ** -0.5, 1.5, (), jnp.float32),
        "output_weight": scatter_about(seeds[6], (H * HD, C), (H * HD) ** -0.5, 0.5),
        "token_weight": scatter_about(seeds[7], (C, CT), C ** -0.5, 0.5),
        "token_grad": scatter_about(own_keys[8], (SAMPLES, NTOK, CT), 4.0, 24.0, ((0, 4), (1, 4))),
    }


EPSILON = 1e-05

def layer_norm(values):
    center = values - lax.optimization_barrier(jnp.mean(values, axis=-1, keepdims=True))
    variance = lax.optimization_barrier(jnp.mean(center * center, axis=-1, keepdims=True))
    inverse = 1.0 / jnp.sqrt(variance + EPSILON)
    return (center * inverse, inverse)

def silu_slope(preact):
    sigma = jax.nn.sigmoid(preact)
    return sigma * (1.0 + preact * (1.0 - sigma))

def rounded(values):
    return lax.optimization_barrier(values.astype(jnp.bfloat16))

def reference(atom_single, token_counts, key_shift, atom_pair, project_weight, bias_weight, output_weight, token_weight, token_grad):
    heads_width = H * HD
    score_scale = HD ** (-0.5)
    atom_ids = jnp.arange(NATOM, dtype=jnp.int32)
    blocks = atom_ids // ATOM_DEV
    within = atom_ids % ATOM_DEV
    token_ends = jnp.cumsum(token_counts, axis=1).astype(jnp.int32)
    local_token = lax.optimization_barrier(jnp.sum((token_ends[blocks] <= within[:, None]).astype(jnp.int32), axis=1)).astype(jnp.int32)
    token_index = (blocks * TOK_DEV + local_token).astype(jnp.int32)
    atom_count = token_counts[blocks, local_token].astype(jnp.float32)
    bias = jnp.einsum('wci,ch->whi', atom_pair.astype(jnp.float32), bias_weight, precision=lax.Precision.HIGHEST).reshape(NWIN, H, QW, KW)
    key_index = (QW * jnp.arange(NWIN, dtype=jnp.int32) - (KW - QW) // 2 + key_shift)[:, None] + jnp.arange(KW, dtype=jnp.int32)[None, :]
    key_valid = (key_index >= 0) & (key_index < NATOM)
    padded_index = (key_index + HALO).astype(jnp.int32)
    flat_index = padded_index.reshape(-1)
    weight32 = project_weight.astype(jnp.float32)

    def sample_step(carry, inputs):
        token_sum, project_sum, pair_sum = carry
        single, upstream = inputs
        single32 = single.astype(jnp.float32)
        normed, inverse = layer_norm(single32)
        normed_half = rounded(normed).astype(jnp.float32)
        projected = jnp.einsum('nc,kcd->knd', normed_half, weight32)
        queries = rounded(projected[0]).astype(jnp.float32)
        keys_all = rounded(projected[1]).astype(jnp.float32)
        values_all = rounded(projected[2]).astype(jnp.float32)
        gate = jax.nn.sigmoid(projected[3])
        key_pad = jnp.pad(keys_all, ((HALO, HALO), (0, 0)))
        value_pad = jnp.pad(values_all, ((HALO, HALO), (0, 0)))
        key_win = key_pad[padded_index].reshape(NWIN, KW, H, HD)
        value_win = value_pad[padded_index].reshape(NWIN, KW, H, HD)
        query_win = queries.reshape(NWIN, QW, H, HD)
        scores = jnp.einsum('wqhd,wkhd->whqk', query_win, key_win) * score_scale + bias
        scores = jnp.where(key_valid[:, None, None, :], scores, -jnp.inf)
        row_top = lax.optimization_barrier(jnp.max(scores, axis=-1, keepdims=True))
        expo = jnp.exp(scores - row_top)
        probs = expo / lax.optimization_barrier(jnp.sum(expo, axis=-1, keepdims=True))
        probs_half = rounded(probs).astype(jnp.float32)
        attended = jnp.einsum('whqk,wkhd->wqhd', probs_half, value_win).reshape(NATOM, heads_width)
        gated = (gate * attended).astype(jnp.bfloat16)
        hidden = (single32 + jnp.dot(gated, output_weight, preferred_element_type=jnp.float32)).astype(jnp.bfloat16)
        preact = jnp.dot(hidden, token_weight, preferred_element_type=jnp.float32)
        picked = upstream[token_index].astype(jnp.float32) / atom_count[:, None]
        slope_grad = (picked * silu_slope(preact)).astype(jnp.bfloat16)
        token_sum = token_sum + jnp.dot(hidden.T, slope_grad, preferred_element_type=jnp.float32)
        hidden_grad = jnp.dot(slope_grad, token_weight.T, preferred_element_type=jnp.float32)
        hidden_half = hidden_grad.astype(jnp.bfloat16)
        gated_grad = jnp.dot(hidden_half, output_weight.T, preferred_element_type=jnp.float32)
        attended_grad = rounded(gated_grad * gate).astype(jnp.float32)
        gate_grad = rounded(gated_grad * attended * gate * (1.0 - gate)).astype(jnp.float32)
        attended_win = attended_grad.reshape(NWIN, QW, H, HD)
        prob_grad = jnp.einsum('wqhd,wkhd->whqk', attended_win, value_win)
        row_total = lax.optimization_barrier(jnp.sum(probs * prob_grad, axis=-1, keepdims=True))
        logit_grad = probs * (prob_grad - row_total)
        logit_half = rounded(logit_grad).astype(jnp.float32)
        query_grad = rounded((jnp.einsum('whqk,wkhd->wqhd', logit_half, key_win) * score_scale).reshape(NATOM, heads_width)).astype(jnp.float32)
        key_grad_win = jnp.einsum('whqk,wqhd->wkhd', logit_half, query_win) * score_scale
        value_grad_win = jnp.einsum('whqk,wqhd->wkhd', probs_half, attended_win)
        key_sum = jnp.zeros((NATOM + 2 * HALO, heads_width), jnp.float32).at[flat_index].add(key_grad_win.reshape(NWIN * KW, heads_width))
        value_sum = jnp.zeros((NATOM + 2 * HALO, heads_width), jnp.float32).at[flat_index].add(value_grad_win.reshape(NWIN * KW, heads_width))
        key_grad = rounded(key_sum[HALO:HALO + NATOM]).astype(jnp.float32)
        value_grad = rounded(value_sum[HALO:HALO + NATOM]).astype(jnp.float32)
        stacked = jnp.stack([query_grad, key_grad, value_grad, gate_grad])
        project_sum = project_sum + jnp.einsum('nc,knd->kcd', normed_half, stacked)
        normed_grad = jnp.einsum('knd,kcd->nc', stacked, weight32)
        ln_grad = inverse * (normed_grad - lax.optimization_barrier(jnp.mean(normed_grad, axis=-1, keepdims=True)) - normed * lax.optimization_barrier(jnp.mean(normed_grad * normed, axis=-1, keepdims=True)))
        single_grad = (hidden_grad + ln_grad).astype(jnp.bfloat16)
        pair_sum = pair_sum + logit_grad.reshape(NWIN, H, QW * KW)
        return ((token_sum, project_sum, pair_sum), single_grad)
    initial = (jnp.zeros((C, CT), jnp.float32), jnp.zeros((4, C, heads_width), jnp.float32), jnp.zeros((NWIN, H, QW * KW), jnp.float32))
    (token_sum, project_sum, pair_sum), single_grad = lax.scan(sample_step, initial, (atom_single, token_grad))
    pair_grad = jnp.einsum('whi,ch->wci', pair_sum, bias_weight, precision=lax.Precision.HIGHEST).astype(jnp.bfloat16)
    return (single_grad, pair_grad, token_sum, project_sum)
```

```python
import functools

import jax
import jax.numpy as jnp
from jax import lax
from jax.experimental import pallas as pl
from jax.experimental.pallas import tpu as pltpu
from jax.sharding import PartitionSpec as P

H = 4
HD = 32
QW = 32
KW = 128
HALO = 64
JIT = 16
EPSILON = 1e-05
MESH = pl.DeviceIdType.MESH
F32 = jnp.float32
BF16 = jnp.bfloat16


def dot(a, b, ca=1, cb=0, precision=None):
    return lax.dot_general(
        a, b, (((ca,), (cb,)), ((), ())), preferred_element_type=F32, precision=precision
    )


def iota(shape, dim):
    return lax.broadcasted_iota(jnp.int32, shape, dim)


def layer_norm(values):
    center = values - jnp.mean(values, axis=-1, keepdims=True)
    variance = jnp.mean(center * center, axis=-1, keepdims=True)
    inverse = 1.0 / jnp.sqrt(variance + EPSILON)
    return (center * inverse, inverse)


def sigmoid(x):
    return 0.5 + 0.5 * jnp.tanh(0.5 * x)


def per_head(values, lane_head):
    total = values[0:QW]
    for h in range(1, H):
        total = jnp.where(lane_head == h, values[h * QW : (h + 1) * QW], total)
    return total


def kernel(
    n_seq,
    n_smp,
    n_rep,
    x_hbm,
    counts_ref,
    shift_ref,
    pair_hbm,
    pw_hbm,
    bw_ref,
    ow_hbm,
    tw_hbm,
    tg_hbm,
    single_out,
    pair_out,
    token_out,
    project_out,
    x_ext,
    pair,
    pw,
    ow,
    tw,
    tg,
    nh,
    nf,
    inv,
    q_s,
    k_s,
    v_s,
    gate_s,
    bias_s,
    prob_s,
    hid_s,
    sg_s,
    hg_s,
    da_s,
    dg_s,
    dq_s,
    dk_s,
    dv_s,
    kv_win,
    acc,
    lacc,
    psend32,
    psend,
    precv,
    tsend,
    t1,
    t2,
    t3,
    wsend,
    w1,
    w2,
    w3,
    hsend,
    hrecv,
    load_sem,
    halo_send,
    halo_recv,
    back_send,
    back_recv,
    pair_send_sem,
    pair_recv_sem,
    t_send_q,
    t_recv_q,
    t_send_z,
    t_recv_z,
    t_send_f,
    t_recv_f,
    w_send_q,
    w_recv_q,
    w_send_z,
    w_recv_z,
    w_send_f,
    w_recv_f,
):
    samples, ext, width = x_ext.shape
    atoms = ext - 2 * HALO
    windows = bias_s.shape[0]
    nq = n_smp * n_rep
    z = lax.axis_index("seq")
    me_q = lax.axis_index("smp") * n_rep + lax.axis_index("rep")
    scale = HD ** (-0.5)

    def seq_peer(offset):
        return {"seq": lax.rem(z + offset, n_seq)}

    def quarter_peer(offset):
        other = lax.rem(me_q + offset, nq)
        return other, {"smp": other // n_rep, "rep": lax.rem(other, n_rep)}

    own = slice(HALO, HALO + atoms)
    loads = [
        pltpu.make_async_copy(source, target, load_sem.at[i])
        for i, (source, target) in enumerate(
            [
                (x_hbm, x_ext.at[:, HALO : HALO + atoms, :]),
                (pw_hbm, pw),
                (pair_hbm, pair),
                (ow_hbm, ow),
                (tw_hbm, tw),
                (tg_hbm, tg),
            ]
        )
    ]
    for load in loads:
        load.start()

    barrier = pltpu.get_barrier_semaphore()
    for k in range(1, n_seq):
        pl.semaphore_signal(barrier, inc=1, device_id=seq_peer(k), device_id_type=MESH)
    for k in range(1, nq):
        pl.semaphore_signal(barrier, inc=1, device_id=quarter_peer(k)[1], device_id_type=MESH)
    pl.semaphore_wait(barrier, n_seq - 1 + nq - 1)

    up = pltpu.make_async_remote_copy(
        src_ref=x_hbm.at[:, atoms - HALO : atoms, :],
        dst_ref=x_ext.at[:, 0:HALO, :],
        send_sem=halo_send.at[0],
        recv_sem=halo_recv.at[0],
        device_id={"seq": jnp.minimum(z + 1, n_seq - 1)},
        device_id_type=MESH,
    )
    down = pltpu.make_async_remote_copy(
        src_ref=x_hbm.at[:, 0:HALO, :],
        dst_ref=x_ext.at[:, HALO + atoms : ext, :],
        send_sem=halo_send.at[1],
        recv_sem=halo_recv.at[1],
        device_id={"seq": jnp.maximum(z - 1, 0)},
        device_id_type=MESH,
    )
    has_up = z < n_seq - 1
    has_down = z > 0

    @pl.when(has_up)
    def _():
        up.start()

    @pl.when(has_down)
    def _():
        down.start()

    @pl.when(z == 0)
    def _():
        x_ext[:, 0:HALO, :] = jnp.zeros((samples, HALO, width), BF16)

    @pl.when(z == n_seq - 1)
    def _():
        x_ext[:, HALO + atoms : ext, :] = jnp.zeros((samples, HALO, width), BF16)

    loads[0].wait()
    loads[1].wait()
    rows = samples * atoms
    normed, inverse = layer_norm(x_ext[:, own, :].reshape(rows, width).astype(F32))
    nf[...] = normed.reshape(samples, atoms, width)
    inv[...] = inverse.reshape(samples, atoms, 1)
    half = normed.astype(BF16)
    nh[:, own, :] = half.reshape(samples, atoms, width)
    q_s[...] = dot(half, pw[0]).astype(BF16).reshape(samples, atoms, width)
    k_s[:, own, :] = dot(half, pw[1]).astype(BF16).reshape(samples, atoms, width)
    v_s[:, own, :] = dot(half, pw[2]).astype(BF16).reshape(samples, atoms, width)
    gate_s[...] = sigmoid(dot(half, pw[3])).reshape(samples, atoms, width)

    pairs_wide = pair.shape[1]
    group = 16
    deep = group * pairs_wide
    bw = bw_ref[...]
    terms = []
    rest = bw
    for _ in range(3):
        term = rest.astype(BF16)
        terms.append(term)
        rest = rest - term.astype(F32)
    spread = (
        jnp.bitwise_and(iota((pairs_wide, deep), 1), pairs_wide - 1) == iota((pairs_wide, deep), 0)
    ).astype(BF16)
    diagonal = iota((group, deep), 1) // pairs_wide == iota((group, deep), 0)
    mixer = []
    for term in terms:
        line = dot(term, spread, 0, 0)
        for h in range(H):
            mixer.append(
                jnp.where(diagonal, jnp.broadcast_to(line[h : h + 1], (group, deep)), 0.0)
            )
    mixer = jnp.concatenate(mixer, axis=0).astype(BF16)
    loads[2].wait()
    key_at = iota((1, KW), 1)
    for w in range(windows):
        first = z * atoms + QW * w - (KW - QW) // 2 + shift_ref[w]
        key_global = first + key_at
        mask = jnp.where((key_global >= 0) & (key_global < n_seq * atoms), 0.0, -1e30)
        for g in range(QW // group):
            stack = jnp.concatenate(
                [pair[w, :, (g * group + r) * KW : (g * group + r + 1) * KW] for r in range(group)],
                axis=0,
            )
            mixed = dot(mixer, stack)
            part = H * group
            mixed = mixed[0:part] + (mixed[part : 2 * part] + mixed[2 * part : 3 * part])
            for h in range(H):
                bias_s[w, h * QW + g * group : h * QW + (g + 1) * group, :] = (
                    mixed[h * group : (h + 1) * group] + mask
                )

    tokens = counts_ref.shape[1]
    counts = counts_ref[...].astype(F32)
    before = (iota((tokens, tokens), 0) < iota((tokens, tokens), 1)).astype(BF16)
    begins = dot(jnp.broadcast_to(counts, (8, tokens)).astype(BF16), before)[0:1]
    place = iota((atoms, tokens), 0).astype(F32)
    member32 = jnp.where((place >= begins) & (place < begins + counts), 1.0, 0.0)
    per_atom = 1.0 / jnp.sum(member32 * counts, axis=1, keepdims=True)
    member = member32.astype(BF16)

    row_head = jnp.right_shift(iota((H * QW, width), 0), 5)
    lane_head = jnp.right_shift(iota((QW, width), 1), 5)
    head_mask = (row_head == jnp.right_shift(iota((H * QW, width), 1), 5)).astype(BF16)

    lacc[...] = jnp.zeros_like(lacc)

    @pl.when(has_down)
    def _():
        up.wait_recv()

    @pl.when(has_up)
    def _():
        down.wait_recv()

    for side in (slice(0, HALO), slice(HALO + atoms, ext)):
        side_normed, _ = layer_norm(x_ext[:, side, :].reshape(samples * HALO, width).astype(F32))
        side_half = side_normed.astype(BF16)
        nh[:, side, :] = side_half.reshape(samples, HALO, width)
        k_s[:, side, :] = dot(side_half, pw[1]).astype(BF16).reshape(samples, HALO, width)
        v_s[:, side, :] = dot(side_half, pw[2]).astype(BF16).reshape(samples, HALO, width)
    for i in (3, 4, 5):
        loads[i].wait()

    moves = []
    weights = []
    for w in range(windows):
        moved = jnp.full((1, width), shift_ref[w], jnp.int32)
        moves.append((moved < 0, moved == 0))
        weights.append(
            [jnp.where(moved == JIT * step, 1.0, 0.0).astype(BF16) for step in (-1, 0, 1)]
        )

    def window_of(ref, s, w):
        total = None
        for step in range(3):
            at = w * QW + step * JIT
            term = ref[s, at : at + KW, :] * weights[w][step]
            total = term if total is None else total + term
        return total

    def moved_back(values, w):
        blank = jnp.zeros((JIT, width), F32)
        low, middle = moves[w]
        return jnp.where(
            low,
            jnp.concatenate([values, blank, blank], axis=0),
            jnp.where(
                middle,
                jnp.concatenate([blank, values, blank], axis=0),
                jnp.concatenate([blank, blank, values], axis=0),
            ),
        )

    def spread_heads(values):
        return jnp.concatenate([values] * H, axis=0) * head_mask

    chunk = 256
    token_width = tw.shape[1]

    def forward(s, carry):
        parts = []
        for w in range(windows):
            keys = window_of(k_s, s, w)
            values = window_of(v_s, s, w)
            kv_win[s, w, 0] = keys
            kv_win[s, w, 1] = values
            queries = spread_heads(q_s[s, w * QW : (w + 1) * QW, :])
            scores = dot(queries, keys, 1, 1) * scale + bias_s[w]
            expo = jnp.exp(scores - jnp.max(scores, axis=-1, keepdims=True))
            probs = expo * (1.0 / jnp.sum(expo, axis=-1, keepdims=True))
            prob_s[s, w] = probs
            parts.append(per_head(dot(probs.astype(BF16), values), lane_head))
        attended = jnp.concatenate(parts, axis=0)
        gate = gate_s[s]
        gated = (gate * attended).astype(BF16)
        hidden = (x_ext[s, own, :].astype(F32) + dot(gated, ow[...])).astype(BF16)
        hid_s[s] = hidden
        hidden_grad = jnp.zeros((atoms, width), F32)
        for b in range(token_width // chunk):
            columns = slice(b * chunk, (b + 1) * chunk)
            weight = tw[:, columns]
            preact = dot(hidden, weight)
            picked = dot(member, tg[s, :, columns]) * per_atom
            sigma = sigmoid(preact)
            slope = (picked * (sigma * (1.0 + preact * (1.0 - sigma)))).astype(BF16)
            sg_s[s, :, columns] = slope
            hidden_grad = hidden_grad + dot(slope, weight, 1, 1)
        hg_s[s] = hidden_grad
        gated_grad = dot(hidden_grad.astype(BF16), ow[...], 1, 1)
        da_s[s] = (gated_grad * gate).astype(BF16)
        dg_s[s] = (gated_grad * attended * gate * (1.0 - gate)).astype(BF16)
        return carry

    lax.fori_loop(0, samples, forward, 0)

    def send_pieces(source, slots, send, recv):
        size = slots.shape[1]
        copies = []
        for k in range(1, nq):
            other, where = quarter_peer(k)
            copies.append(
                pltpu.make_async_remote_copy(
                    src_ref=source.at[pl.ds(pl.multiple_of(other * size, 16), size), :],
                    dst_ref=slots.at[me_q],
                    send_sem=send.at[k],
                    recv_sem=recv.at[k],
                    device_id=where,
                    device_id_type=MESH,
                )
            )
        for copy in copies:
            copy.start()
        slots[me_q] = source[pl.ds(pl.multiple_of(me_q * size, 16), size), :]
        return copies

    def send_along(first, slots, send, recv, arrived):
        for copy in arrived:
            copy.wait_recv()
        total = first[0].astype(F32)
        for i in range(1, nq):
            total = total + first[i].astype(F32)
        slots[z] = total.astype(BF16)
        copies = [
            pltpu.make_async_remote_copy(
                src_ref=slots.at[z],
                dst_ref=slots.at[z],
                send_sem=send.at[k],
                recv_sem=recv.at[k],
                device_id=seq_peer(k),
                device_id_type=MESH,
            )
            for k in range(1, n_seq)
        ]
        for copy in copies:
            copy.start()
        return copies

    def send_back(second, target, send, recv, arrived):
        for copy in arrived:
            copy.wait_recv()
        size = second.shape[1]
        total = second[0].astype(F32)
        for i in range(1, n_seq):
            total = total + second[i].astype(F32)
        mine = pl.ds(pl.multiple_of(me_q * size, 16), size)
        target[mine, :] = total.astype(BF16)
        copies = [
            pltpu.make_async_remote_copy(
                src_ref=target.at[mine, :],
                dst_ref=target.at[mine, :],
                send_sem=send.at[k],
                recv_sem=recv.at[k],
                device_id=quarter_peer(k)[1],
                device_id_type=MESH,
            )
            for k in range(1, nq)
        ]
        for copy in copies:
            copy.start()
        return copies

    all_hidden = hid_s[...].reshape(rows, width)
    for b in range(token_width // chunk):
        part = dot(all_hidden, sg_s[:, :, b * chunk : (b + 1) * chunk].reshape(rows, chunk), 0, 0)
        for i in range(chunk // width):
            at = (b * (chunk // width) + i) * width
            tsend[at : at + width, :] = part[:, i * width : (i + 1) * width].astype(BF16)
    token_pieces = send_pieces(tsend, t1, t_send_q, t_recv_q)

    def backward(s, carry):
        acc[...] = jnp.zeros_like(acc)
        parts = []
        for w in range(windows):
            keys = kv_win[s, w, 0]
            values = kv_win[s, w, 1]
            queries = spread_heads(q_s[s, w * QW : (w + 1) * QW, :])
            upstream = spread_heads(da_s[s, w * QW : (w + 1) * QW, :])
            probs = prob_s[s, w]
            prob_grad = dot(upstream, values, 1, 1)
            weighted = probs * prob_grad
            logit_grad = weighted - probs * jnp.sum(weighted, axis=-1, keepdims=True)
            lacc[w] += logit_grad
            logit_half = logit_grad.astype(BF16)
            parts.append(per_head(dot(logit_half, keys), lane_head))
            reach = slice(w * QW, w * QW + KW + QW)
            acc[0, reach, :] += moved_back(dot(logit_half, queries, 0, 0), w)
            acc[1, reach, :] += moved_back(dot(probs.astype(BF16), upstream, 0, 0), w)
        dq_s[s] = (jnp.concatenate(parts, axis=0) * scale).astype(BF16)
        dk_s[s] = (acc[0] * scale).astype(BF16)
        dv_s[s] = acc[1].astype(BF16)
        return carry

    lax.fori_loop(0, samples // 2, backward, 0)
    token_along = send_along(t1, t2, t_send_z, t_recv_z, token_pieces)
    lax.fori_loop(samples // 2, samples, backward, 0)

    for i, side in enumerate((slice(HALO + atoms, ext), slice(0, HALO))):
        side_grad = dot(dk_s[:, side, :].reshape(samples * HALO, width), pw[1], 1, 1) + dot(
            dv_s[:, side, :].reshape(samples * HALO, width), pw[2], 1, 1
        )
        hsend[i] = side_grad.astype(BF16).reshape(samples, HALO, width)
    back_up = pltpu.make_async_remote_copy(
        src_ref=hsend.at[0],
        dst_ref=hrecv.at[0],
        send_sem=back_send.at[0],
        recv_sem=back_recv.at[0],
        device_id={"seq": jnp.minimum(z + 1, n_seq - 1)},
        device_id_type=MESH,
    )
    back_down = pltpu.make_async_remote_copy(
        src_ref=hsend.at[1],
        dst_ref=hrecv.at[1],
        send_sem=back_send.at[1],
        recv_sem=back_recv.at[1],
        device_id={"seq": jnp.maximum(z - 1, 0)},
        device_id_type=MESH,
    )

    @pl.when(has_up)
    def _():
        back_up.start()

    @pl.when(has_down)
    def _():
        back_down.start()

    @pl.when(z == 0)
    def _():
        hrecv[0] = jnp.zeros((samples, HALO, width), BF16)

    @pl.when(z == n_seq - 1)
    def _():
        hrecv[1] = jnp.zeros((samples, HALO, width), BF16)

    own_half = nh[:, own, :].reshape(rows, width)
    all_half = nh[...].reshape(samples * ext, width)
    wsend[0:width, :] = dot(own_half, dq_s[...].reshape(rows, width), 0, 0).astype(BF16)
    wsend[width : 2 * width, :] = dot(
        all_half, dk_s[...].reshape(samples * ext, width), 0, 0
    ).astype(BF16)
    wsend[2 * width : 3 * width, :] = dot(
        all_half, dv_s[...].reshape(samples * ext, width), 0, 0
    ).astype(BF16)
    wsend[3 * width : 4 * width, :] = dot(own_half, dg_s[...].reshape(rows, width), 0, 0).astype(
        BF16
    )
    project_pieces = send_pieces(wsend, w1, w_send_q, w_recv_q)

    rows_q = QW // nq
    for j in range(nq):
        for w in range(windows):
            for h in range(H):
                at = (w * H + h) * rows_q
                psend32[j, at : at + rows_q, :] = lacc[
                    w, h * QW + j * rows_q : h * QW + (j + 1) * rows_q, :
                ]
    psend[...] = psend32[...].astype(BF16)
    pair_copies = []
    for k in range(1, nq):
        other, where = quarter_peer(k)
        pair_copies.append(
            pltpu.make_async_remote_copy(
                src_ref=psend.at[other],
                dst_ref=precv.at[me_q],
                send_sem=pair_send_sem.at[k],
                recv_sem=pair_recv_sem.at[k],
                device_id=where,
                device_id_type=MESH,
            )
        )
    for copy in pair_copies:
        copy.start()
    precv[me_q] = psend[me_q]

    token_back = send_back(t2, t3, t_send_f, t_recv_f, token_along)

    own_grad = (
        dot(dq_s[...].reshape(rows, width), pw[0], 1, 1)
        + dot(dk_s[:, own, :].reshape(rows, width), pw[1], 1, 1)
        + dot(dv_s[:, own, :].reshape(rows, width), pw[2], 1, 1)
        + dot(dg_s[...].reshape(rows, width), pw[3], 1, 1)
    ).reshape(samples, atoms, width)

    project_along = send_along(w1, w2, w_send_z, w_recv_z, project_pieces)

    @pl.when(has_down)
    def _():
        back_up.wait_recv()

    @pl.when(has_up)
    def _():
        back_down.wait_recv()

    arrived = jnp.concatenate([hrecv[0], hrecv[1]], axis=1).astype(F32)
    normed_grad = own_grad + arrived
    normed = nf[...]
    ln_grad = inv[...] * (
        normed_grad
        - jnp.mean(normed_grad, axis=-1, keepdims=True)
        - normed * jnp.mean(normed_grad * normed, axis=-1, keepdims=True)
    )
    single_out[...] = (hg_s[...] + ln_grad).astype(BF16)

    for copy in pair_copies:
        copy.wait_recv()
    heads = precv[0].astype(F32)
    for i in range(1, nq):
        heads = heads + precv[i].astype(F32)
    tall, deep = rows_q * pairs_wide, H * rows_q
    lift = (
        jnp.bitwise_and(iota((tall, pairs_wide), 0), pairs_wide - 1) == iota((tall, pairs_wide), 1)
    ).astype(F32)
    widen = (iota((H, deep), 1) // rows_q == iota((H, deep), 0)).astype(F32)
    highest = lax.Precision.HIGHEST
    mix_back = dot(dot(lift, bw, precision=highest), widen, precision=highest)
    same = iota((tall, deep), 0) // pairs_wide == jnp.bitwise_and(
        iota((tall, deep), 1), rows_q - 1
    )
    mix_back = jnp.where(same, mix_back, 0.0)
    for w in range(windows):
        result = dot(mix_back, heads[w * deep : (w + 1) * deep], precision=highest).astype(BF16)
        for r in range(rows_q):
            pair_out[w, :, r * KW : (r + 1) * KW] = result[r * pairs_wide : (r + 1) * pairs_wide]

    project_back = send_back(w2, w3, w_send_f, w_recv_f, project_along)
    for copy in token_back:
        copy.wait_recv()
    for b in range(token_width // width):
        token_out[:, b * width : (b + 1) * width] = t3[b * width : (b + 1) * width, :].astype(F32)
    for copy in project_back:
        copy.wait_recv()
    for k in range(4):
        project_out[k] = w3[k * width : (k + 1) * width, :].astype(F32)

    for copies in (
        token_pieces,
        token_along,
        token_back,
        project_pieces,
        project_along,
        project_back,
        pair_copies,
    ):
        for copy in copies:
            copy.wait_send()

    @pl.when(has_up)
    def _():
        up.wait_send()
        back_up.wait_send()

    @pl.when(has_down)
    def _():
        down.wait_send()
        back_down.wait_send()


def solution(mesh):
    n_seq, n_smp, n_rep = (mesh.shape["seq"], mesh.shape["smp"], mesh.shape["rep"])
    nq = n_smp * n_rep

    def on_device(x, counts, shift, pair, pw, bw, ow, tw, tg):
        samples, atoms, width = x.shape
        ext = atoms + 2 * HALO
        windows, pairs_wide, spots = pair.shape
        token_width = tw.shape[1]
        any_space = pl.BlockSpec(memory_space=pl.ANY)
        vmem = pl.BlockSpec(memory_space=pltpu.VMEM)
        smem = pl.BlockSpec(memory_space=pltpu.SMEM)
        rows_q = QW // nq
        t_rows = token_width
        w_rows = 4 * width
        per_atom = (samples, atoms, width)
        per_ext = (samples, ext, width)
        square = (windows, H * QW, KW)
        dma = pltpu.SemaphoreType.DMA
        scratch = [
            pltpu.VMEM(per_ext, BF16),
            pltpu.VMEM(pair.shape, BF16),
            pltpu.VMEM(pw.shape, BF16),
            pltpu.VMEM(ow.shape, BF16),
            pltpu.VMEM(tw.shape, BF16),
            pltpu.VMEM(tg.shape, BF16),
            pltpu.VMEM(per_ext, BF16),
            pltpu.VMEM(per_atom, F32),
            pltpu.VMEM((samples, atoms, 1), F32),
            pltpu.VMEM(per_atom, BF16),
            pltpu.VMEM(per_ext, BF16),
            pltpu.VMEM(per_ext, BF16),
            pltpu.VMEM(per_atom, F32),
            pltpu.VMEM(square, F32),
            pltpu.VMEM((samples,) + square, F32),
            pltpu.VMEM(per_atom, BF16),
            pltpu.VMEM((samples, atoms, token_width), BF16),
            pltpu.VMEM(per_atom, F32),
            pltpu.VMEM(per_atom, BF16),
            pltpu.VMEM(per_atom, BF16),
            pltpu.VMEM(per_atom, BF16),
            pltpu.VMEM(per_ext, BF16),
            pltpu.VMEM(per_ext, BF16),
            pltpu.VMEM((samples, windows, 2, KW, width), BF16),
            pltpu.VMEM((2, ext, width), F32),
            pltpu.VMEM(square, F32),
            pltpu.VMEM((nq, windows * H * rows_q, KW), F32),
            pltpu.VMEM((nq, windows * H * rows_q, KW), BF16),
            pltpu.VMEM((nq, windows * H * rows_q, KW), BF16),
            pltpu.VMEM((t_rows, width), BF16),
            pltpu.VMEM((nq, t_rows // nq, width), BF16),
            pltpu.VMEM((n_seq, t_rows // nq, width), BF16),
            pltpu.VMEM((t_rows, width), BF16),
            pltpu.VMEM((w_rows, width), BF16),
            pltpu.VMEM((nq, w_rows // nq, width), BF16),
            pltpu.VMEM((n_seq, w_rows // nq, width), BF16),
            pltpu.VMEM((w_rows, width), BF16),
            pltpu.VMEM((2, samples, HALO, width), BF16),
            pltpu.VMEM((2, samples, HALO, width), BF16),
            dma((6,)),
        ]
        scratch += [dma((2,))] * 4
        scratch += [dma((nq,))] * 2
        scratch += [dma((n,)) for n in (nq, nq, n_seq, n_seq, nq, nq)] * 2
        return pl.pallas_call(
            functools.partial(kernel, n_seq, n_smp, n_rep),
            out_shape=(
                jax.ShapeDtypeStruct(x.shape, BF16),
                jax.ShapeDtypeStruct((windows, pairs_wide, spots // nq), BF16),
                jax.ShapeDtypeStruct(tw.shape, F32),
                jax.ShapeDtypeStruct(pw.shape, F32),
            ),
            in_specs=[
                any_space,
                vmem,
                smem,
                any_space,
                any_space,
                vmem,
                any_space,
                any_space,
                any_space,
            ],
            out_specs=(vmem,) * 4,
            scratch_shapes=scratch,
            compiler_params=pltpu.CompilerParams(
                collective_id=0, has_side_effects=True, vmem_limit_bytes=40 * 1024 * 1024
            ),
        )(x, counts, shift, pair, pw, bw, ow, tw, tg)

    in_specs = (
        P(("grp", "smp", "rep"), "seq", None),
        P(("grp", "seq"), None),
        P(("grp", "seq")),
        P(("grp", "seq"), None, None),
        P(),
        P(),
        P(),
        P(),
        P(("grp", "smp", "rep"), "seq", None),
    )
    out_specs = (
        P(("grp", "smp", "rep"), "seq", None),
        P(("grp", "seq"), None, ("smp", "rep")),
        P("grp", None),
        P("grp", None, None),
    )
    return jax.shard_map(
        on_device, mesh=mesh, in_specs=in_specs, out_specs=out_specs, check_vma=False
    )
```

```python
import functools

import jax
import jax.numpy as jnp
from jax import lax
from jax.experimental import pallas as pl
from jax.experimental.pallas import tpu as pltpu
from jax.sharding import PartitionSpec as P

H = 4
HD = 32
QW = 32
KW = 128
HALO = 64
JIT = 16
EPSILON = 1e-05
MESH = pl.DeviceIdType.MESH
F32 = jnp.float32
BF16 = jnp.bfloat16


def dot(a, b, ca=1, cb=0, precision=None):
    return lax.dot_general(
        a, b, (((ca,), (cb,)), ((), ())), preferred_element_type=F32, precision=precision
    )


def iota(shape, dim):
    return lax.broadcasted_iota(jnp.int32, shape, dim)


def layer_norm(values):
    center = values - jnp.mean(values, axis=-1, keepdims=True)
    variance = jnp.mean(center * center, axis=-1, keepdims=True)
    inverse = 1.0 / jnp.sqrt(variance + EPSILON)
    return (center * inverse, inverse)


def sigmoid(x):
    return 0.5 + 0.5 * jnp.tanh(0.5 * x)


def per_head(values, lane_head):
    total = values[0:QW]
    for h in range(1, H):
        total = jnp.where(lane_head == h, values[h * QW : (h + 1) * QW], total)
    return total


def kernel(
    n_seq,
    n_smp,
    n_rep,
    x_hbm,
    counts_ref,
    shift_ref,
    pair_hbm,
    pw_hbm,
    bw_ref,
    ow_hbm,
    tw_hbm,
    tg_hbm,
    single_out,
    pair_out,
    token_out,
    project_out,
    x_ext,
    pair,
    pw,
    ow,
    tw,
    tg,
    nh,
    nf,
    inv,
    q_s,
    k_s,
    v_s,
    gate_s,
    bias_s,
    prob_s,
    att_s,
    sg_s,
    hg_s,
    da_s,
    dqg_s,
    dkv_s,
    kv_win,
    acc,
    lacc,
    psend32,
    psend,
    precv,
    tsend,
    t1,
    t2,
    t3,
    wsend,
    w1,
    w2,
    w3,
    hsend,
    hrecv,
    load_sem,
    halo_send,
    halo_recv,
    back_send,
    back_recv,
    pair_send_sem,
    pair_recv_sem,
    t_send_q,
    t_recv_q,
    t_send_z,
    t_recv_z,
    t_send_f,
    t_recv_f,
    w_send_q,
    w_recv_q,
    w_send_z,
    w_recv_z,
    w_send_f,
    w_recv_f,
):
    samples, ext, width = x_ext.shape
    atoms = ext - 2 * HALO
    windows = bias_s.shape[0]
    nq = n_smp * n_rep
    z = lax.axis_index("seq")
    me_q = lax.axis_index("smp") * n_rep + lax.axis_index("rep")
    scale = HD ** (-0.5)

    def seq_peer(offset):
        return {"seq": lax.rem(z + offset, n_seq)}

    def quarter_peer(offset):
        other = lax.rem(me_q + offset, nq)
        return other, {"smp": other // n_rep, "rep": lax.rem(other, n_rep)}

    own = slice(HALO, HALO + atoms)
    loads = [
        pltpu.make_async_copy(source, target, load_sem.at[i])
        for i, (source, target) in enumerate(
            [
                (x_hbm, x_ext.at[:, HALO : HALO + atoms, :]),
                (pw_hbm.at[0], pw.at[:, 0:width]),
                (pw_hbm.at[3], pw.at[:, width : 2 * width]),
                (pw_hbm.at[1], pw.at[:, 2 * width : 3 * width]),
                (pw_hbm.at[2], pw.at[:, 3 * width : 4 * width]),
                (pair_hbm, pair),
                (ow_hbm, ow),
                (tw_hbm, tw),
                (tg_hbm, tg),
            ]
        )
    ]
    for load in loads:
        load.start()

    barrier = pltpu.get_barrier_semaphore()
    for k in range(1, n_seq):
        pl.semaphore_signal(barrier, inc=1, device_id=seq_peer(k), device_id_type=MESH)
    for k in range(1, nq):
        pl.semaphore_signal(barrier, inc=1, device_id=quarter_peer(k)[1], device_id_type=MESH)
    pl.semaphore_wait(barrier, n_seq - 1 + nq - 1)

    up = pltpu.make_async_remote_copy(
        src_ref=x_hbm.at[:, atoms - HALO : atoms, :],
        dst_ref=x_ext.at[:, 0:HALO, :],
        send_sem=halo_send.at[0],
        recv_sem=halo_recv.at[0],
        device_id={"seq": jnp.minimum(z + 1, n_seq - 1)},
        device_id_type=MESH,
    )
    down = pltpu.make_async_remote_copy(
        src_ref=x_hbm.at[:, 0:HALO, :],
        dst_ref=x_ext.at[:, HALO + atoms : ext, :],
        send_sem=halo_send.at[1],
        recv_sem=halo_recv.at[1],
        device_id={"seq": jnp.maximum(z - 1, 0)},
        device_id_type=MESH,
    )
    has_up = z < n_seq - 1
    has_down = z > 0

    @pl.when(has_up)
    def _():
        up.start()

    @pl.when(has_down)
    def _():
        down.start()

    @pl.when(z == 0)
    def _():
        x_ext[:, 0:HALO, :] = jnp.zeros((samples, HALO, width), BF16)

    @pl.when(z == n_seq - 1)
    def _():
        x_ext[:, HALO + atoms : ext, :] = jnp.zeros((samples, HALO, width), BF16)

    for i in range(5):
        loads[i].wait()
    rows = samples * atoms
    normed, inverse = layer_norm(x_ext[:, own, :].reshape(rows, width).astype(F32))
    nf[...] = normed.reshape(samples, atoms, width)
    inv[...] = inverse.reshape(samples, atoms, 1)
    half = normed.astype(BF16)
    nh[:, own, :] = half.reshape(samples, atoms, width)
    wide = (samples, atoms, width)
    projected = dot(half, pw[...])
    q_s[...] = projected[:, 0:width].astype(BF16).reshape(wide)
    gate_s[...] = sigmoid(projected[:, width : 2 * width]).reshape(wide)
    k_s[:, own, :] = projected[:, 2 * width : 3 * width].astype(BF16).reshape(wide)
    v_s[:, own, :] = projected[:, 3 * width :].astype(BF16).reshape(wide)

    pairs_wide = pair.shape[1]
    group = 16
    deep = group * pairs_wide
    bw = bw_ref[...]
    terms = []
    rest = bw
    for _ in range(3):
        term = rest.astype(BF16)
        terms.append(term)
        rest = rest - term.astype(F32)
    spread = (
        jnp.bitwise_and(iota((pairs_wide, deep), 1), pairs_wide - 1) == iota((pairs_wide, deep), 0)
    ).astype(BF16)
    diagonal = iota((group, deep), 1) // pairs_wide == iota((group, deep), 0)
    mixer = []
    for term in terms:
        line = dot(term, spread)
        for h in range(H):
            mixer.append(
                jnp.where(diagonal, jnp.broadcast_to(line[h : h + 1], (group, deep)), 0.0)
            )
    mixer = jnp.concatenate(mixer, axis=0).astype(BF16)
    loads[5].wait()
    key_at = iota((1, KW), 1)
    for w in range(windows):
        first = z * atoms + QW * w - (KW - QW) // 2 + shift_ref[w]
        key_global = first + key_at
        mask = jnp.where((key_global >= 0) & (key_global < n_seq * atoms), 0.0, -1e30)
        for g in range(QW // group):
            stack = jnp.concatenate(
                [pair[w, :, (g * group + r) * KW : (g * group + r + 1) * KW] for r in range(group)],
                axis=0,
            )
            mixed = dot(mixer, stack)
            part = H * group
            mixed = mixed[0:part] + (mixed[part : 2 * part] + mixed[2 * part : 3 * part])
            for h in range(H):
                bias_s[w, h * QW + g * group : h * QW + (g + 1) * group, :] = (
                    mixed[h * group : (h + 1) * group] + mask
                )

    tokens = counts_ref.shape[1]
    counts = counts_ref[...].astype(F32)
    before = (iota((tokens, tokens), 0) < iota((tokens, tokens), 1)).astype(BF16)
    begins = dot(jnp.broadcast_to(counts, (8, tokens)).astype(BF16), before)[0:1]
    place = iota((atoms, tokens), 0).astype(F32)
    member32 = jnp.where((place >= begins) & (place < begins + counts), 1.0, 0.0)
    per_atom = 1.0 / jnp.sum(member32 * counts, axis=1, keepdims=True)
    member = member32.astype(BF16)

    row_head = jnp.right_shift(iota((H * QW, width), 0), 5)
    lane_head = jnp.right_shift(iota((QW, width), 1), 5)
    head_mask = (row_head == jnp.right_shift(iota((H * QW, width), 1), 5)).astype(BF16)

    lacc[...] = jnp.zeros_like(lacc)

    rows_q = QW // nq
    tall, flat = rows_q * pairs_wide, H * rows_q
    lift = (
        jnp.bitwise_and(iota((tall, pairs_wide), 0), pairs_wide - 1) == iota((tall, pairs_wide), 1)
    ).astype(F32)
    widen = (iota((H, flat), 1) // rows_q == iota((H, flat), 0)).astype(F32)
    highest = lax.Precision.HIGHEST
    mix_back = dot(dot(lift, bw, 1, 1, precision=highest), widen, precision=highest)
    same = iota((tall, flat), 0) // pairs_wide == jnp.bitwise_and(
        iota((tall, flat), 1), rows_q - 1
    )
    mix_back = jnp.where(same, mix_back, 0.0)

    @pl.when(has_down)
    def _():
        up.wait_recv()

    @pl.when(has_up)
    def _():
        down.wait_recv()

    for side in (slice(0, HALO), slice(HALO + atoms, ext)):
        side_normed, _ = layer_norm(x_ext[:, side, :].reshape(samples * HALO, width).astype(F32))
        side_half = side_normed.astype(BF16)
        nh[:, side, :] = side_half.reshape(samples, HALO, width)
        side_kv = dot(side_half, pw[:, 2 * width :])
        k_s[:, side, :] = side_kv[:, 0:width].astype(BF16).reshape(samples, HALO, width)
        v_s[:, side, :] = side_kv[:, width:].astype(BF16).reshape(samples, HALO, width)
    for i in (6, 7, 8):
        loads[i].wait()

    moves = []
    weights = []
    for w in range(windows):
        moved = jnp.full((1, width), shift_ref[w], jnp.int32)
        moves.append((moved < 0, moved == 0))
        weights.append(
            [jnp.where(moved == JIT * step, 1.0, 0.0).astype(BF16) for step in (-1, 0, 1)]
        )

    def window_of(ref, s, w):
        total = None
        for step in range(3):
            at = w * QW + step * JIT
            term = ref[s, at : at + KW, :] * weights[w][step]
            total = term if total is None else total + term
        return total

    def moved_back(values, w):
        blank = jnp.zeros((JIT, width), F32)
        low, middle = moves[w]
        return jnp.where(
            low,
            jnp.concatenate([values, blank, blank], axis=0),
            jnp.where(
                middle,
                jnp.concatenate([blank, values, blank], axis=0),
                jnp.concatenate([blank, blank, values], axis=0),
            ),
        )

    def spread_heads(values):
        return jnp.concatenate([values] * H, axis=0) * head_mask

    chunk = 256
    token_width = tw.shape[1]

    def attend(s, carry):
        keys = [window_of(k_s, s, w) for w in range(windows)]
        values = [window_of(v_s, s, w) for w in range(windows)]
        queries = [spread_heads(q_s[s, w * QW : (w + 1) * QW, :]) for w in range(windows)]
        scores = [dot(queries[w], keys[w], 1, 1) for w in range(windows)]
        scores = [scores[w] * scale + bias_s[w] for w in range(windows)]
        tops = [jnp.max(scores[w], axis=-1, keepdims=True) for w in range(windows)]
        expos = [jnp.exp(scores[w] - tops[w]) for w in range(windows)]
        sums = [jnp.sum(expos[w], axis=-1, keepdims=True) for w in range(windows)]
        probs = [expos[w] * (1.0 / sums[w]) for w in range(windows)]
        outs = [dot(probs[w].astype(BF16), values[w]) for w in range(windows)]
        for w in range(windows):
            kv_win[s, w, 0] = keys[w]
            kv_win[s, w, 1] = values[w]
            prob_s[s, w] = probs[w]
            att_s[s, w * QW : (w + 1) * QW, :] = per_head(outs[w], lane_head)
        return carry

    lax.fori_loop(0, samples, attend, 0)

    def send_pieces(source, slots, send, recv):
        size = slots.shape[1]
        copies = []
        for k in range(1, nq):
            other, where = quarter_peer(k)
            copies.append(
                pltpu.make_async_remote_copy(
                    src_ref=source.at[pl.ds(pl.multiple_of(other * size, 16), size), :],
                    dst_ref=slots.at[me_q],
                    send_sem=send.at[k],
                    recv_sem=recv.at[k],
                    device_id=where,
                    device_id_type=MESH,
                )
            )
        for copy in copies:
            copy.start()
        slots[me_q] = source[pl.ds(pl.multiple_of(me_q * size, 16), size), :]
        return copies

    def send_along(first, slots, send, recv, arrived):
        for copy in arrived:
            copy.wait_recv()
        total = first[0].astype(F32)
        for i in range(1, nq):
            total = total + first[i].astype(F32)
        slots[z] = total.astype(BF16)
        copies = [
            pltpu.make_async_remote_copy(
                src_ref=slots.at[z],
                dst_ref=slots.at[z],
                send_sem=send.at[k],
                recv_sem=recv.at[k],
                device_id=seq_peer(k),
                device_id_type=MESH,
            )
            for k in range(1, n_seq)
        ]
        for copy in copies:
            copy.start()
        return copies

    def send_back(second, target, send, recv, arrived):
        for copy in arrived:
            copy.wait_recv()
        size = second.shape[1]
        total = second[0].astype(F32)
        for i in range(1, n_seq):
            total = total + second[i].astype(F32)
        mine = pl.ds(pl.multiple_of(me_q * size, 16), size)
        target[mine, :] = total.astype(BF16)
        copies = [
            pltpu.make_async_remote_copy(
                src_ref=target.at[mine, :],
                dst_ref=target.at[mine, :],
                send_sem=send.at[k],
                recv_sem=recv.at[k],
                device_id=quarter_peer(k)[1],
                device_id_type=MESH,
            )
            for k in range(1, nq)
        ]
        for copy in copies:
            copy.start()
        return copies

    attended = att_s[...].reshape(rows, width)
    gate = gate_s[...].reshape(rows, width)
    gated = (gate * attended).astype(BF16)
    hidden = x_ext[:, own, :].reshape(rows, width).astype(F32) + dot(gated, ow[...])
    hidden = hidden.astype(BF16)
    for b in range(token_width // chunk):
        columns = slice(b * chunk, (b + 1) * chunk)
        preact = dot(hidden, tw[:, columns])
        picked = jnp.concatenate(
            [dot(member, tg[s, :, columns]) * per_atom for s in range(samples)], axis=0
        )
        sigma = sigmoid(preact)
        sg_s[:, columns] = (picked * (sigma * (1.0 + preact * (1.0 - sigma)))).astype(BF16)
    token_part = dot(hidden, sg_s[...], 0, 0)
    for b in range(token_width // width):
        tsend[b * width : (b + 1) * width, :] = token_part[:, b * width : (b + 1) * width].astype(
            BF16
        )
    token_pieces = send_pieces(tsend, t1, t_send_q, t_recv_q)

    hidden_grad = dot(sg_s[...], tw[...], 1, 1)
    hg_s[...] = hidden_grad.reshape(wide)
    gated_grad = dot(hidden_grad.astype(BF16), ow[...], 1, 1)
    gate = gate_s[...].reshape(rows, width)
    attended = att_s[...].reshape(rows, width)
    da_s[...] = (gated_grad * gate).astype(BF16).reshape(wide)
    dqg_s[:, :, width:] = (
        (gated_grad * attended * gate * (1.0 - gate)).astype(BF16).reshape(wide)
    )

    def backward(s, carry):
        each = range(windows)
        values = [kv_win[s, w, 1] for w in each]
        upstream = [spread_heads(da_s[s, w * QW : (w + 1) * QW, :]) for w in each]
        prob_grad = [dot(upstream[w], values[w], 1, 1) for w in each]
        value_grad = [dot(prob_s[s, w].astype(BF16), upstream[w], 0, 0) for w in each]
        weighted = [prob_s[s, w] * prob_grad[w] for w in each]
        sums = [jnp.sum(weighted[w], axis=-1, keepdims=True) for w in each]
        logit_grad = [weighted[w] - prob_s[s, w] * sums[w] for w in each]
        logit_half = [logit_grad[w].astype(BF16) for w in each]
        query_grad = [dot(logit_half[w], kv_win[s, w, 0]) for w in each]
        queries = [spread_heads(q_s[s, w * QW : (w + 1) * QW, :]) for w in each]
        key_grad = [dot(logit_half[w], queries[w], 0, 0) for w in each]
        acc[...] = jnp.zeros_like(acc)
        for w in each:
            lacc[w] += logit_grad[w]
            reach = slice(w * QW, w * QW + KW + QW)
            acc[0, reach, :] += moved_back(key_grad[w], w)
            acc[1, reach, :] += moved_back(value_grad[w], w)
            dqg_s[s, w * QW : (w + 1) * QW, 0:width] = (
                per_head(query_grad[w], lane_head) * scale
            ).astype(BF16)
        dkv_s[s, :, 0:width] = (acc[0] * scale).astype(BF16)
        dkv_s[s, :, width:] = acc[1].astype(BF16)
        return carry

    lax.fori_loop(0, samples // 2, backward, 0)
    token_along = send_along(t1, t2, t_send_z, t_recv_z, token_pieces)
    lax.fori_loop(samples // 2, samples, backward, 0)

    own_half = nh[:, own, :].reshape(rows, width)
    all_half = nh[...].reshape(samples * ext, width)
    query_gate = dot(own_half, dqg_s[...].reshape(rows, 2 * width), 0, 0).astype(BF16)
    key_value = dot(all_half, dkv_s[...].reshape(samples * ext, 2 * width), 0, 0).astype(BF16)
    wsend[0:width, :] = query_gate[:, 0:width]
    wsend[width : 2 * width, :] = key_value[:, 0:width]
    wsend[2 * width : 3 * width, :] = key_value[:, width:]
    wsend[3 * width :, :] = query_gate[:, width:]
    project_pieces = send_pieces(wsend, w1, w_send_q, w_recv_q)

    for i, side in enumerate((slice(HALO + atoms, ext), slice(0, HALO))):
        side_grad = dot(
            dkv_s[:, side, :].reshape(samples * HALO, 2 * width), pw[:, 2 * width :], 1, 1
        )
        hsend[i] = side_grad.astype(BF16).reshape(samples, HALO, width)
    back_up = pltpu.make_async_remote_copy(
        src_ref=hsend.at[0],
        dst_ref=hrecv.at[0],
        send_sem=back_send.at[0],
        recv_sem=back_recv.at[0],
        device_id={"seq": jnp.minimum(z + 1, n_seq - 1)},
        device_id_type=MESH,
    )
    back_down = pltpu.make_async_remote_copy(
        src_ref=hsend.at[1],
        dst_ref=hrecv.at[1],
        send_sem=back_send.at[1],
        recv_sem=back_recv.at[1],
        device_id={"seq": jnp.maximum(z - 1, 0)},
        device_id_type=MESH,
    )

    @pl.when(has_up)
    def _():
        back_up.start()

    @pl.when(has_down)
    def _():
        back_down.start()

    @pl.when(z == 0)
    def _():
        hrecv[0] = jnp.zeros((samples, HALO, width), BF16)

    @pl.when(z == n_seq - 1)
    def _():
        hrecv[1] = jnp.zeros((samples, HALO, width), BF16)

    for j in range(nq):
        for w in range(windows):
            for h in range(H):
                at = (w * H + h) * rows_q
                psend32[j, at : at + rows_q, :] = lacc[
                    w, h * QW + j * rows_q : h * QW + (j + 1) * rows_q, :
                ]
    psend[...] = psend32[...].astype(BF16)
    pair_copies = []
    for k in range(1, nq):
        other, where = quarter_peer(k)
        pair_copies.append(
            pltpu.make_async_remote_copy(
                src_ref=psend.at[other],
                dst_ref=precv.at[me_q],
                send_sem=pair_send_sem.at[k],
                recv_sem=pair_recv_sem.at[k],
                device_id=where,
                device_id_type=MESH,
            )
        )
    for copy in pair_copies:
        copy.start()
    precv[me_q] = psend[me_q]

    token_back = send_back(t2, t3, t_send_f, t_recv_f, token_along)

    own_grad = (
        dot(dqg_s[...].reshape(rows, 2 * width), pw[:, 0 : 2 * width], 1, 1)
        + dot(dkv_s[:, own, :].reshape(rows, 2 * width), pw[:, 2 * width :], 1, 1)
    ).reshape(samples, atoms, width)

    project_along = send_along(w1, w2, w_send_z, w_recv_z, project_pieces)

    @pl.when(has_down)
    def _():
        back_up.wait_recv()

    @pl.when(has_up)
    def _():
        back_down.wait_recv()

    arrived = jnp.concatenate([hrecv[0], hrecv[1]], axis=1).astype(F32)
    normed_grad = own_grad + arrived
    normed = nf[...]
    ln_grad = inv[...] * (
        normed_grad
        - jnp.mean(normed_grad, axis=-1, keepdims=True)
        - normed * jnp.mean(normed_grad * normed, axis=-1, keepdims=True)
    )
    single_out[...] = (hg_s[...] + ln_grad).astype(BF16)

    for copy in pair_copies:
        copy.wait_recv()
    heads = precv[0].astype(F32)
    for i in range(1, nq):
        heads = heads + precv[i].astype(F32)
    for w in range(windows):
        result = dot(mix_back, heads[w * flat : (w + 1) * flat], precision=highest).astype(BF16)
        for r in range(rows_q):
            pair_out[w, :, r * KW : (r + 1) * KW] = result[r * pairs_wide : (r + 1) * pairs_wide]

    project_back = send_back(w2, w3, w_send_f, w_recv_f, project_along)
    for copy in token_back:
        copy.wait_recv()
    for b in range(token_width // width):
        token_out[:, b * width : (b + 1) * width] = t3[b * width : (b + 1) * width, :].astype(F32)
    for copy in project_back:
        copy.wait_recv()
    for k in range(4):
        project_out[k] = w3[k * width : (k + 1) * width, :].astype(F32)

    for copies in (
        token_pieces,
        token_along,
        token_back,
        project_pieces,
        project_along,
        project_back,
        pair_copies,
    ):
        for copy in copies:
            copy.wait_send()

    @pl.when(has_up)
    def _():
        up.wait_send()
        back_up.wait_send()

    @pl.when(has_down)
    def _():
        down.wait_send()
        back_down.wait_send()


def solution(mesh):
    n_seq, n_smp, n_rep = (mesh.shape["seq"], mesh.shape["smp"], mesh.shape["rep"])
    nq = n_smp * n_rep

    def on_device(x, counts, shift, pair, pw, bw, ow, tw, tg):
        samples, atoms, width = x.shape
        ext = atoms + 2 * HALO
        windows, pairs_wide, spots = pair.shape
        token_width = tw.shape[1]
        any_space = pl.BlockSpec(memory_space=pl.ANY)
        vmem = pl.BlockSpec(memory_space=pltpu.VMEM)
        smem = pl.BlockSpec(memory_space=pltpu.SMEM)
        rows_q = QW // nq
        t_rows = token_width
        w_rows = 4 * width
        per_atom = (samples, atoms, width)
        per_ext = (samples, ext, width)
        square = (windows, H * QW, KW)
        dma = pltpu.SemaphoreType.DMA
        scratch = [
            pltpu.VMEM(per_ext, BF16),
            pltpu.VMEM(pair.shape, BF16),
            pltpu.VMEM((width, 4 * width), BF16),
            pltpu.VMEM(ow.shape, BF16),
            pltpu.VMEM(tw.shape, BF16),
            pltpu.VMEM(tg.shape, BF16),
            pltpu.VMEM(per_ext, BF16),
            pltpu.VMEM(per_atom, F32),
            pltpu.VMEM((samples, atoms, 1), F32),
            pltpu.VMEM(per_atom, BF16),
            pltpu.VMEM(per_ext, BF16),
            pltpu.VMEM(per_ext, BF16),
            pltpu.VMEM(per_atom, F32),
            pltpu.VMEM(square, F32),
            pltpu.VMEM((samples,) + square, F32),
            pltpu.VMEM(per_atom, F32),
            pltpu.VMEM((samples * atoms, token_width), BF16),
            pltpu.VMEM(per_atom, F32),
            pltpu.VMEM(per_atom, BF16),
            pltpu.VMEM((samples, atoms, 2 * width), BF16),
            pltpu.VMEM((samples, ext, 2 * width), BF16),
            pltpu.VMEM((samples, windows, 2, KW, width), BF16),
            pltpu.VMEM((2, ext, width), F32),
            pltpu.VMEM(square, F32),
            pltpu.VMEM((nq, windows * H * rows_q, KW), F32),
            pltpu.VMEM((nq, windows * H * rows_q, KW), BF16),
            pltpu.VMEM((nq, windows * H * rows_q, KW), BF16),
            pltpu.VMEM((t_rows, width), BF16),
            pltpu.VMEM((nq, t_rows // nq, width), BF16),
            pltpu.VMEM((n_seq, t_rows // nq, width), BF16),
            pltpu.VMEM((t_rows, width), BF16),
            pltpu.VMEM((w_rows, width), BF16),
            pltpu.VMEM((nq, w_rows // nq, width), BF16),
            pltpu.VMEM((n_seq, w_rows // nq, width), BF16),
            pltpu.VMEM((w_rows, width), BF16),
            pltpu.VMEM((2, samples, HALO, width), BF16),
            pltpu.VMEM((2, samples, HALO, width), BF16),
            dma((9,)),
        ]
        scratch += [dma((2,))] * 4
        scratch += [dma((nq,))] * 2
        scratch += [dma((n,)) for n in (nq, nq, n_seq, n_seq, nq, nq)] * 2
        return pl.pallas_call(
            functools.partial(kernel, n_seq, n_smp, n_rep),
            out_shape=(
                jax.ShapeDtypeStruct(x.shape, BF16),
                jax.ShapeDtypeStruct((windows, pairs_wide, spots // nq), BF16),
                jax.ShapeDtypeStruct(tw.shape, F32),
                jax.ShapeDtypeStruct(pw.shape, F32),
            ),
            in_specs=[
                any_space,
                vmem,
                smem,
                any_space,
                any_space,
                vmem,
                any_space,
                any_space,
                any_space,
            ],
            out_specs=(vmem,) * 4,
            scratch_shapes=scratch,
            compiler_params=pltpu.CompilerParams(
                collective_id=0, has_side_effects=True, vmem_limit_bytes=60 * 1024 * 1024
            ),
        )(x, counts, shift, pair, pw, bw.T, ow, tw, tg)

    in_specs = (
        P(("grp", "smp", "rep"), "seq", None),
        P(("grp", "seq"), None),
        P(("grp", "seq")),
        P(("grp", "seq"), None, None),
        P(),
        P(),
        P(),
        P(),
        P(("grp", "smp", "rep"), "seq", None),
    )
    out_specs = (
        P(("grp", "smp", "rep"), "seq", None),
        P(("grp", "seq"), None, ("smp", "rep")),
        P("grp", None),
        P("grp", None, None),
    )
    return jax.shard_map(
        on_device, mesh=mesh, in_specs=in_specs, out_specs=out_specs, check_vma=False
    )
```

```python
import functools

import jax
import jax.numpy as jnp
from jax import lax
from jax.experimental import pallas as pl
from jax.experimental.pallas import tpu as pltpu
from jax.sharding import PartitionSpec as P

H = 4
HD = 32
QW = 32
KW = 128
HALO = 64
JIT = 16
EPSILON = 1e-05
MESH = pl.DeviceIdType.MESH
F32 = jnp.float32
BF16 = jnp.bfloat16


def dot(a, b, ca=1, cb=0, precision=None):
    return lax.dot_general(
        a, b, (((ca,), (cb,)), ((), ())), preferred_element_type=F32, precision=precision
    )


def iota(shape, dim):
    return lax.broadcasted_iota(jnp.int32, shape, dim)


def layer_norm(values):
    center = values - jnp.mean(values, axis=-1, keepdims=True)
    variance = jnp.mean(center * center, axis=-1, keepdims=True)
    inverse = 1.0 / jnp.sqrt(variance + EPSILON)
    return (center * inverse, inverse)


def sigmoid(x):
    return 0.5 + 0.5 * jnp.tanh(0.5 * x)


def per_head(values, lane_head):
    total = values[0:QW]
    for h in range(1, H):
        total = jnp.where(lane_head == h, values[h * QW : (h + 1) * QW], total)
    return total


def kernel(
    n_seq,
    n_smp,
    n_rep,
    x_hbm,
    counts_ref,
    shift_ref,
    pair_hbm,
    pw_hbm,
    bw_ref,
    ow_hbm,
    tw_hbm,
    tg_hbm,
    single_out,
    pair_out,
    token_out,
    project_out,
    x_ext,
    pair,
    pw,
    ow,
    tw,
    tg,
    nh,
    nf,
    inv,
    q_s,
    k_s,
    v_s,
    gate_s,
    bias_s,
    prob_s,
    att_s,
    sg_s,
    hg_s,
    da_s,
    dqg_s,
    dkv_s,
    kv_win,
    acc,
    lacc,
    psend32,
    psend,
    precv,
    tsend,
    t1,
    t2,
    t3,
    wsend,
    w1,
    w2,
    w3,
    hsend,
    hrecv,
    load_sem,
    halo_send,
    halo_recv,
    back_send,
    back_recv,
    pair_send_sem,
    pair_recv_sem,
    t_send_q,
    t_recv_q,
    t_send_z,
    t_recv_z,
    t_send_f,
    t_recv_f,
    w_send_q,
    w_recv_q,
    w_send_z,
    w_recv_z,
    w_send_f,
    w_recv_f,
):
    samples, ext, width = x_ext.shape
    atoms = ext - 2 * HALO
    windows = bias_s.shape[0]
    nq = n_smp * n_rep
    z = lax.axis_index("seq")
    me_q = lax.axis_index("smp") * n_rep + lax.axis_index("rep")
    scale = HD ** (-0.5)

    def seq_peer(offset):
        return {"seq": lax.rem(z + offset, n_seq)}

    def quarter_peer(offset):
        other = lax.rem(me_q + offset, nq)
        return other, {"smp": other // n_rep, "rep": lax.rem(other, n_rep)}

    own = slice(HALO, HALO + atoms)
    loads = [
        pltpu.make_async_copy(source, target, load_sem.at[i])
        for i, (source, target) in enumerate(
            [
                (x_hbm, x_ext.at[:, HALO : HALO + atoms, :]),
                (pw_hbm.at[0], pw.at[:, 0:width]),
                (pw_hbm.at[3], pw.at[:, width : 2 * width]),
                (pw_hbm.at[1], pw.at[:, 2 * width : 3 * width]),
                (pw_hbm.at[2], pw.at[:, 3 * width : 4 * width]),
                (pair_hbm, pair),
                (ow_hbm, ow),
                (tw_hbm, tw),
                (tg_hbm, tg),
            ]
        )
    ]
    for load in loads:
        load.start()

    barrier = pltpu.get_barrier_semaphore()
    for k in range(1, n_seq):
        pl.semaphore_signal(barrier, inc=1, device_id=seq_peer(k), device_id_type=MESH)
    for k in range(1, nq):
        pl.semaphore_signal(barrier, inc=1, device_id=quarter_peer(k)[1], device_id_type=MESH)
    pl.semaphore_wait(barrier, n_seq - 1 + nq - 1)

    up = pltpu.make_async_remote_copy(
        src_ref=x_hbm.at[:, atoms - HALO : atoms, :],
        dst_ref=x_ext.at[:, 0:HALO, :],
        send_sem=halo_send.at[0],
        recv_sem=halo_recv.at[0],
        device_id={"seq": jnp.minimum(z + 1, n_seq - 1)},
        device_id_type=MESH,
    )
    down = pltpu.make_async_remote_copy(
        src_ref=x_hbm.at[:, 0:HALO, :],
        dst_ref=x_ext.at[:, HALO + atoms : ext, :],
        send_sem=halo_send.at[1],
        recv_sem=halo_recv.at[1],
        device_id={"seq": jnp.maximum(z - 1, 0)},
        device_id_type=MESH,
    )
    has_up = z < n_seq - 1
    has_down = z > 0

    @pl.when(has_up)
    def _():
        up.start()

    @pl.when(has_down)
    def _():
        down.start()

    @pl.when(z == 0)
    def _():
        x_ext[:, 0:HALO, :] = jnp.zeros((samples, HALO, width), BF16)

    @pl.when(z == n_seq - 1)
    def _():
        x_ext[:, HALO + atoms : ext, :] = jnp.zeros((samples, HALO, width), BF16)

    for i in range(5):
        loads[i].wait()
    rows = samples * atoms
    normed, inverse = layer_norm(x_ext[:, own, :].reshape(rows, width).astype(F32))
    nf[...] = normed.reshape(samples, atoms, width)
    inv[...] = inverse.reshape(samples, atoms, 1)
    half = normed.astype(BF16)
    nh[:, own, :] = half.reshape(samples, atoms, width)
    wide = (samples, atoms, width)
    projected = dot(half, pw[...])
    q_s[...] = projected[:, 0:width].astype(BF16).reshape(wide)
    gate_s[...] = sigmoid(projected[:, width : 2 * width]).reshape(wide)
    k_s[:, own, :] = projected[:, 2 * width : 3 * width].astype(BF16).reshape(wide)
    v_s[:, own, :] = projected[:, 3 * width :].astype(BF16).reshape(wide)

    pairs_wide = pair.shape[1]
    group = 16
    deep = group * pairs_wide
    bw = bw_ref[...]
    terms = []
    rest = bw
    for _ in range(3):
        term = rest.astype(BF16)
        terms.append(term)
        rest = rest - term.astype(F32)
    spread = (
        jnp.bitwise_and(iota((pairs_wide, deep), 1), pairs_wide - 1) == iota((pairs_wide, deep), 0)
    ).astype(BF16)
    diagonal = iota((group, deep), 1) // pairs_wide == iota((group, deep), 0)
    mixer = []
    for term in terms:
        line = dot(term, spread)
        for h in range(H):
            mixer.append(
                jnp.where(diagonal, jnp.broadcast_to(line[h : h + 1], (group, deep)), 0.0)
            )
    mixer = jnp.concatenate(mixer, axis=0).astype(BF16)
    loads[5].wait()
    key_at = iota((1, KW), 1)
    for w in range(windows):
        first = z * atoms + QW * w - (KW - QW) // 2 + shift_ref[w]
        key_global = first + key_at
        mask = jnp.where((key_global >= 0) & (key_global < n_seq * atoms), 0.0, -1e30)
        for g in range(QW // group):
            stack = jnp.concatenate(
                [pair[w, :, (g * group + r) * KW : (g * group + r + 1) * KW] for r in range(group)],
                axis=0,
            )
            mixed = dot(mixer, stack)
            part = H * group
            mixed = mixed[0:part] + (mixed[part : 2 * part] + mixed[2 * part : 3 * part])
            for h in range(H):
                bias_s[w, h * QW + g * group : h * QW + (g + 1) * group, :] = (
                    mixed[h * group : (h + 1) * group] + mask
                )

    tokens = counts_ref.shape[1]
    counts = counts_ref[...].astype(F32)
    before = (iota((tokens, tokens), 0) < iota((tokens, tokens), 1)).astype(BF16)
    begins = dot(jnp.broadcast_to(counts, (8, tokens)).astype(BF16), before)[0:1]
    place = iota((atoms, tokens), 0).astype(F32)
    member32 = jnp.where((place >= begins) & (place < begins + counts), 1.0, 0.0)
    per_atom = 1.0 / jnp.sum(member32 * counts, axis=1, keepdims=True)
    member = member32.astype(BF16)

    row_head = jnp.right_shift(iota((H * QW, width), 0), 5)
    lane_head = jnp.right_shift(iota((QW, width), 1), 5)
    head_mask = (row_head == jnp.right_shift(iota((H * QW, width), 1), 5)).astype(BF16)

    lacc[...] = jnp.zeros_like(lacc)

    rows_q = QW // nq
    tall, flat = rows_q * pairs_wide, H * rows_q
    lift = (
        jnp.bitwise_and(iota((tall, pairs_wide), 0), pairs_wide - 1) == iota((tall, pairs_wide), 1)
    ).astype(F32)
    widen = (iota((H, flat), 1) // rows_q == iota((H, flat), 0)).astype(F32)
    highest = lax.Precision.HIGHEST
    mix_back = dot(dot(lift, bw, 1, 1, precision=highest), widen, precision=highest)
    same = iota((tall, flat), 0) // pairs_wide == jnp.bitwise_and(
        iota((tall, flat), 1), rows_q - 1
    )
    mix_back = jnp.where(same, mix_back, 0.0)

    @pl.when(has_down)
    def _():
        up.wait_recv()

    @pl.when(has_up)
    def _():
        down.wait_recv()

    for side in (slice(0, HALO), slice(HALO + atoms, ext)):
        side_normed, _ = layer_norm(x_ext[:, side, :].reshape(samples * HALO, width).astype(F32))
        side_half = side_normed.astype(BF16)
        nh[:, side, :] = side_half.reshape(samples, HALO, width)
        side_kv = dot(side_half, pw[:, 2 * width :])
        k_s[:, side, :] = side_kv[:, 0:width].astype(BF16).reshape(samples, HALO, width)
        v_s[:, side, :] = side_kv[:, width:].astype(BF16).reshape(samples, HALO, width)
    for i in (6, 7, 8):
        loads[i].wait()

    moves = []
    weights = []
    for w in range(windows):
        moved = jnp.full((1, width), shift_ref[w], jnp.int32)
        moves.append((moved < 0, moved == 0))
        weights.append(
            [jnp.where(moved == JIT * step, 1.0, 0.0).astype(BF16) for step in (-1, 0, 1)]
        )

    def window_of(ref, s, w):
        total = None
        for step in range(3):
            at = w * QW + step * JIT
            term = ref[s, at : at + KW, :] * weights[w][step]
            total = term if total is None else total + term
        return total

    def moved_back(values, w):
        blank = jnp.zeros((JIT, width), F32)
        low, middle = moves[w]
        return jnp.where(
            low,
            jnp.concatenate([values, blank, blank], axis=0),
            jnp.where(
                middle,
                jnp.concatenate([blank, values, blank], axis=0),
                jnp.concatenate([blank, blank, values], axis=0),
            ),
        )

    def spread_heads(values):
        return jnp.concatenate([values] * H, axis=0) * head_mask

    chunk = 256
    token_width = tw.shape[1]

    def attend(s, carry):
        keys = [window_of(k_s, s, w) for w in range(windows)]
        values = [window_of(v_s, s, w) for w in range(windows)]
        queries = [spread_heads(q_s[s, w * QW : (w + 1) * QW, :]) for w in range(windows)]
        scores = [dot(queries[w], keys[w], 1, 1) for w in range(windows)]
        scores = [scores[w] * scale + bias_s[w] for w in range(windows)]
        tops = [jnp.max(scores[w], axis=-1, keepdims=True) for w in range(windows)]
        expos = [jnp.exp(scores[w] - tops[w]) for w in range(windows)]
        sums = [jnp.sum(expos[w], axis=-1, keepdims=True) for w in range(windows)]
        probs = [expos[w] * (1.0 / sums[w]) for w in range(windows)]
        outs = [dot(probs[w].astype(BF16), values[w]) for w in range(windows)]
        for w in range(windows):
            kv_win[s, w, 0] = keys[w]
            kv_win[s, w, 1] = values[w]
            prob_s[s, w] = probs[w]
            att_s[s, w * QW : (w + 1) * QW, :] = per_head(outs[w], lane_head)
        return carry

    lax.fori_loop(0, samples, attend, 0)

    def send_pieces(source, slots, send, recv):
        size = slots.shape[1]
        copies = []
        for k in range(1, nq):
            other, where = quarter_peer(k)
            copies.append(
                pltpu.make_async_remote_copy(
                    src_ref=source.at[pl.ds(pl.multiple_of(other * size, 16), size), :],
                    dst_ref=slots.at[me_q],
                    send_sem=send.at[k],
                    recv_sem=recv.at[k],
                    device_id=where,
                    device_id_type=MESH,
                )
            )
        for copy in copies:
            copy.start()
        slots[me_q] = source[pl.ds(pl.multiple_of(me_q * size, 16), size), :]
        return copies

    def send_along(first, slots, send, recv, arrived):
        for copy in arrived:
            copy.wait_recv()
        total = first[0].astype(F32)
        for i in range(1, nq):
            total = total + first[i].astype(F32)
        slots[z] = total.astype(BF16)
        copies = [
            pltpu.make_async_remote_copy(
                src_ref=slots.at[z],
                dst_ref=slots.at[z],
                send_sem=send.at[k],
                recv_sem=recv.at[k],
                device_id=seq_peer(k),
                device_id_type=MESH,
            )
            for k in range(1, n_seq)
        ]
        for copy in copies:
            copy.start()
        return copies

    def send_back(second, target, send, recv, arrived):
        for copy in arrived:
            copy.wait_recv()
        size = second.shape[1]
        total = second[0].astype(F32)
        for i in range(1, n_seq):
            total = total + second[i].astype(F32)
        mine = pl.ds(pl.multiple_of(me_q * size, 16), size)
        target[mine, :] = total.astype(BF16)
        copies = [
            pltpu.make_async_remote_copy(
                src_ref=target.at[mine, :],
                dst_ref=target.at[mine, :],
                send_sem=send.at[k],
                recv_sem=recv.at[k],
                device_id=quarter_peer(k)[1],
                device_id_type=MESH,
            )
            for k in range(1, nq)
        ]
        for copy in copies:
            copy.start()
        return copies

    attended = att_s[...].reshape(rows, width)
    gate = gate_s[...].reshape(rows, width)
    gated = (gate * attended).astype(BF16)
    hidden = x_ext[:, own, :].reshape(rows, width).astype(F32) + dot(gated, ow[...])
    hidden = hidden.astype(BF16)
    for b in range(token_width // chunk):
        columns = slice(b * chunk, (b + 1) * chunk)
        preact = dot(hidden, tw[:, columns])
        picked = jnp.concatenate(
            [dot(member, tg[s, :, columns]) * per_atom for s in range(samples)], axis=0
        )
        sigma = sigmoid(preact)
        sg_s[:, columns] = (picked * (sigma * (1.0 + preact * (1.0 - sigma)))).astype(BF16)
    token_part = dot(hidden, sg_s[...], 0, 0)
    for b in range(token_width // width):
        tsend[b * width : (b + 1) * width, :] = token_part[:, b * width : (b + 1) * width].astype(
            BF16
        )
    token_pieces = send_pieces(tsend, t1, t_send_q, t_recv_q)

    hidden_grad = dot(sg_s[...], tw[...], 1, 1)
    hg_s[...] = hidden_grad.reshape(wide)
    gated_grad = dot(hidden_grad.astype(BF16), ow[...], 1, 1)
    gate = gate_s[...].reshape(rows, width)
    attended = att_s[...].reshape(rows, width)
    da_s[...] = (gated_grad * gate).astype(BF16).reshape(wide)
    dqg_s[:, :, width:] = (
        (gated_grad * attended * gate * (1.0 - gate)).astype(BF16).reshape(wide)
    )

    def backward(s, carry):
        each = range(windows)
        values = [kv_win[s, w, 1] for w in each]
        upstream = [spread_heads(da_s[s, w * QW : (w + 1) * QW, :]) for w in each]
        prob_grad = [dot(upstream[w], values[w], 1, 1) for w in each]
        value_grad = [dot(prob_s[s, w].astype(BF16), upstream[w], 0, 0) for w in each]
        weighted = [prob_s[s, w] * prob_grad[w] for w in each]
        sums = [jnp.sum(weighted[w], axis=-1, keepdims=True) for w in each]
        logit_grad = [weighted[w] - prob_s[s, w] * sums[w] for w in each]
        logit_half = [logit_grad[w].astype(BF16) for w in each]
        query_grad = [dot(logit_half[w], kv_win[s, w, 0]) for w in each]
        queries = [spread_heads(q_s[s, w * QW : (w + 1) * QW, :]) for w in each]
        key_grad = [dot(logit_half[w], queries[w], 0, 0) for w in each]
        acc[...] = jnp.zeros_like(acc)
        for w in each:
            lacc[w] += logit_grad[w]
            reach = slice(w * QW, w * QW + KW + QW)
            acc[0, reach, :] += moved_back(key_grad[w], w)
            acc[1, reach, :] += moved_back(value_grad[w], w)
            dqg_s[s, w * QW : (w + 1) * QW, 0:width] = (
                per_head(query_grad[w], lane_head) * scale
            ).astype(BF16)
        dkv_s[s, :, 0:width] = (acc[0] * scale).astype(BF16)
        dkv_s[s, :, width:] = acc[1].astype(BF16)
        return carry

    lax.fori_loop(0, samples, backward, 0)
    token_along = send_along(t1, t2, t_send_z, t_recv_z, token_pieces)

    own_half = nh[:, own, :].reshape(rows, width)
    all_half = nh[...].reshape(samples * ext, width)
    query_gate = dot(own_half, dqg_s[...].reshape(rows, 2 * width), 0, 0).astype(BF16)
    key_value = dot(all_half, dkv_s[...].reshape(samples * ext, 2 * width), 0, 0).astype(BF16)
    wsend[0:width, :] = query_gate[:, 0:width]
    wsend[width : 2 * width, :] = key_value[:, 0:width]
    wsend[2 * width : 3 * width, :] = key_value[:, width:]
    wsend[3 * width :, :] = query_gate[:, width:]
    project_pieces = send_pieces(wsend, w1, w_send_q, w_recv_q)

    for i, side in enumerate((slice(HALO + atoms, ext), slice(0, HALO))):
        side_grad = dot(
            dkv_s[:, side, :].reshape(samples * HALO, 2 * width), pw[:, 2 * width :], 1, 1
        )
        hsend[i] = side_grad.astype(BF16).reshape(samples, HALO, width)
    back_up = pltpu.make_async_remote_copy(
        src_ref=hsend.at[0],
        dst_ref=hrecv.at[0],
        send_sem=back_send.at[0],
        recv_sem=back_recv.at[0],
        device_id={"seq": jnp.minimum(z + 1, n_seq - 1)},
        device_id_type=MESH,
    )
    back_down = pltpu.make_async_remote_copy(
        src_ref=hsend.at[1],
        dst_ref=hrecv.at[1],
        send_sem=back_send.at[1],
        recv_sem=back_recv.at[1],
        device_id={"seq": jnp.maximum(z - 1, 0)},
        device_id_type=MESH,
    )

    @pl.when(has_up)
    def _():
        back_up.start()

    @pl.when(has_down)
    def _():
        back_down.start()

    @pl.when(z == 0)
    def _():
        hrecv[0] = jnp.zeros((samples, HALO, width), BF16)

    @pl.when(z == n_seq - 1)
    def _():
        hrecv[1] = jnp.zeros((samples, HALO, width), BF16)

    for j in range(nq):
        for w in range(windows):
            for h in range(H):
                at = (w * H + h) * rows_q
                psend32[j, at : at + rows_q, :] = lacc[
                    w, h * QW + j * rows_q : h * QW + (j + 1) * rows_q, :
                ]
    psend[...] = psend32[...].astype(BF16)
    pair_copies = []
    for k in range(1, nq):
        other, where = quarter_peer(k)
        pair_copies.append(
            pltpu.make_async_remote_copy(
                src_ref=psend.at[other],
                dst_ref=precv.at[me_q],
                send_sem=pair_send_sem.at[k],
                recv_sem=pair_recv_sem.at[k],
                device_id=where,
                device_id_type=MESH,
            )
        )
    for copy in pair_copies:
        copy.start()
    precv[me_q] = psend[me_q]

    own_grad = (
        dot(dqg_s[...].reshape(rows, 2 * width), pw[:, 0 : 2 * width], 1, 1)
        + dot(dkv_s[:, own, :].reshape(rows, 2 * width), pw[:, 2 * width :], 1, 1)
    ).reshape(samples, atoms, width)

    project_along = send_along(w1, w2, w_send_z, w_recv_z, project_pieces)

    @pl.when(has_down)
    def _():
        back_up.wait_recv()

    @pl.when(has_up)
    def _():
        back_down.wait_recv()

    arrived = jnp.concatenate([hrecv[0], hrecv[1]], axis=1).astype(F32)
    normed_grad = own_grad + arrived
    normed = nf[...]
    ln_grad = inv[...] * (
        normed_grad
        - jnp.mean(normed_grad, axis=-1, keepdims=True)
        - normed * jnp.mean(normed_grad * normed, axis=-1, keepdims=True)
    )
    single_out[...] = (hg_s[...] + ln_grad).astype(BF16)

    token_back = send_back(t2, t3, t_send_f, t_recv_f, token_along)

    for copy in pair_copies:
        copy.wait_recv()
    heads = precv[0].astype(F32)
    for i in range(1, nq):
        heads = heads + precv[i].astype(F32)
    for w in range(windows):
        result = dot(mix_back, heads[w * flat : (w + 1) * flat], precision=highest).astype(BF16)
        for r in range(rows_q):
            pair_out[w, :, r * KW : (r + 1) * KW] = result[r * pairs_wide : (r + 1) * pairs_wide]

    project_back = send_back(w2, w3, w_send_f, w_recv_f, project_along)
    for copy in token_back:
        copy.wait_recv()
    for b in range(token_width // width):
        token_out[:, b * width : (b + 1) * width] = t3[b * width : (b + 1) * width, :].astype(F32)
    for copy in project_back:
        copy.wait_recv()
    for k in range(4):
        project_out[k] = w3[k * width : (k + 1) * width, :].astype(F32)

    for copies in (
        token_pieces,
        token_along,
        token_back,
        project_pieces,
        project_along,
        project_back,
        pair_copies,
    ):
        for copy in copies:
            copy.wait_send()

    @pl.when(has_up)
    def _():
        up.wait_send()
        back_up.wait_send()

    @pl.when(has_down)
    def _():
        down.wait_send()
        back_down.wait_send()


def solution(mesh):
    n_seq, n_smp, n_rep = (mesh.shape["seq"], mesh.shape["smp"], mesh.shape["rep"])
    nq = n_smp * n_rep

    def on_device(x, counts, shift, pair, pw, bw, ow, tw, tg):
        samples, atoms, width = x.shape
        ext = atoms + 2 * HALO
        windows, pairs_wide, spots = pair.shape
        token_width = tw.shape[1]
        any_space = pl.BlockSpec(memory_space=pl.ANY)
        vmem = pl.BlockSpec(memory_space=pltpu.VMEM)
        smem = pl.BlockSpec(memory_space=pltpu.SMEM)
        rows_q = QW // nq
        t_rows = token_width
        w_rows = 4 * width
        per_atom = (samples, atoms, width)
        per_ext = (samples, ext, width)
        square = (windows, H * QW, KW)
        dma = pltpu.SemaphoreType.DMA
        scratch = [
            pltpu.VMEM(per_ext, BF16),
            pltpu.VMEM(pair.shape, BF16),
            pltpu.VMEM((width, 4 * width), BF16),
            pltpu.VMEM(ow.shape, BF16),
            pltpu.VMEM(tw.shape, BF16),
            pltpu.VMEM(tg.shape, BF16),
            pltpu.VMEM(per_ext, BF16),
            pltpu.VMEM(per_atom, F32),
            pltpu.VMEM((samples, atoms, 1), F32),
            pltpu.VMEM(per_atom, BF16),
            pltpu.VMEM(per_ext, BF16),
            pltpu.VMEM(per_ext, BF16),
            pltpu.VMEM(per_atom, F32),
            pltpu.VMEM(square, F32),
            pltpu.VMEM((samples,) + square, F32),
            pltpu.VMEM(per_atom, F32),
            pltpu.VMEM((samples * atoms, token_width), BF16),
            pltpu.VMEM(per_atom, F32),
            pltpu.VMEM(per_atom, BF16),
            pltpu.VMEM((samples, atoms, 2 * width), BF16),
            pltpu.VMEM((samples, ext, 2 * width), BF16),
            pltpu.VMEM((samples, windows, 2, KW, width), BF16),
            pltpu.VMEM((2, ext, width), F32),
            pltpu.VMEM(square, F32),
            pltpu.VMEM((nq, windows * H * rows_q, KW), F32),
            pltpu.VMEM((nq, windows * H * rows_q, KW), BF16),
            pltpu.VMEM((nq, windows * H * rows_q, KW), BF16),
            pltpu.VMEM((t_rows, width), BF16),
            pltpu.VMEM((nq, t_rows // nq, width), BF16),
            pltpu.VMEM((n_seq, t_rows // nq, width), BF16),
            pltpu.VMEM((t_rows, width), BF16),
            pltpu.VMEM((w_rows, width), BF16),
            pltpu.VMEM((nq, w_rows // nq, width), BF16),
            pltpu.VMEM((n_seq, w_rows // nq, width), BF16),
            pltpu.VMEM((w_rows, width), BF16),
            pltpu.VMEM((2, samples, HALO, width), BF16),
            pltpu.VMEM((2, samples, HALO, width), BF16),
            dma((9,)),
        ]
        scratch += [dma((2,))] * 4
        scratch += [dma((nq,))] * 2
        scratch += [dma((n,)) for n in (nq, nq, n_seq, n_seq, nq, nq)] * 2
        return pl.pallas_call(
            functools.partial(kernel, n_seq, n_smp, n_rep),
            out_shape=(
                jax.ShapeDtypeStruct(x.shape, BF16),
                jax.ShapeDtypeStruct((windows, pairs_wide, spots // nq), BF16),
                jax.ShapeDtypeStruct(tw.shape, F32),
                jax.ShapeDtypeStruct(pw.shape, F32),
            ),
            in_specs=[
                any_space,
                vmem,
                smem,
                any_space,
                any_space,
                vmem,
                any_space,
                any_space,
                any_space,
            ],
            out_specs=(vmem,) * 4,
            scratch_shapes=scratch,
            compiler_params=pltpu.CompilerParams(
                collective_id=0, has_side_effects=True, vmem_limit_bytes=60 * 1024 * 1024
            ),
        )(x, counts, shift, pair, pw, bw.T, ow, tw, tg)

    in_specs = (
        P(("grp", "smp", "rep"), "seq", None),
        P(("grp", "seq"), None),
        P(("grp", "seq")),
        P(("grp", "seq"), None, None),
        P(),
        P(),
        P(),
        P(),
        P(("grp", "smp", "rep"), "seq", None),
    )
    out_specs = (
        P(("grp", "smp", "rep"), "seq", None),
        P(("grp", "seq"), None, ("smp", "rep")),
        P("grp", None),
        P("grp", None, None),
    )
    return jax.shard_map(
        on_device, mesh=mesh, in_specs=in_specs, out_specs=out_specs, check_vma=False
    )
```
